256 devices in a mesh: dp: 8 (over y, core), mp: 32 (over z, x).
Axes of the slice: x: 4, y: 4, z: 8, core: 2. Of those that a mesh axis runs over, the one named last changes fastest.
Arguments:
- gradient: bfloat16 [8, 6144, 6144], P('dp', 'mp'), may hold values from -6 to 6
- error: bfloat16 [8, 6144, 6144], P('dp', 'mp'), may hold values from -6 to 6
- momentum: bfloat16 [6144, 6144], P('mp'), may hold values from -6 to 6
- q_init: float32 [6144, 128], P('mp'), may hold values from -6 to 6
Outputs:
- new_error: bfloat16 [8, 6144, 6144], P('dp', 'mp')
- new_momentum: bfloat16 [6144, 6144], P('mp')
- new_q: float32 [6144, 128], P('mp')
The draws below stay inside these ranges and needn't reach their ends.
All inputs are finite; a program needn't handle non-finite values.
Results may differ from the reference program's by a relative error of at most 0.0012.
Values sent between devices are 32-bit elements; how exact they have to be, the bound alone decides.
No kernel may reach another device: no remote copies, remote signals or barrier semaphores. Data moves between devices by JAX's collectives and lax.ppermute only.
A program may use at most 64 MiB of HBM per device.

```python
import jax
import jax.numpy as jnp
from jax import lax

COLS = 6144
RANK = 128
ITERS = 2
ROWS = 6144
REPL = 8


def block_levels(own_key, shape, shards, smallest, top_value):
    gain = 1.0
    for position, blocks in shards:
        draws = jax.random.uniform(jax.random.fold_in(jax.random.fold_in(own_key, 6), position), (blocks,), jnp.float32, smallest / len(shards), top_value / len(shards))
        gain = gain * jnp.repeat(jnp.exp(draws), shape[position] // blocks).reshape((-1,) + (1,) * (len(shape) - 1 - position))
    return gain


def normal_values(own_key, dims, spread, limit, split=(), dtype=jnp.bfloat16):
    level = block_levels(own_key, dims, split, -0.22, 0.18) if split else 1.0
    values = jax.random.normal(own_key, dims, jnp.float32) * spread * level
    return jnp.minimum(jnp.maximum(values, -limit), limit).astype(dtype)


def setup_inputs(seed: int = 0) -> dict:
    key_list = jax.random.split(jax.random.key(seed), 5)
    return {
        "gradient": normal_values(key_list[0], (REPL, ROWS, COLS), 1.0, 6.0, ((0, 8), (1, 32))),
        "error": normal_values(key_list[1], (REPL, ROWS, COLS), 0.5, 6.0, ((0, 8), (1, 32))),
        "momentum": normal_values(key_list[2], (ROWS, COLS), 1.0, 6.0, ((0, 32),)),
        "q_init": normal_values(key_list[3], (COLS, RANK), 1.0, 6.0, ((0, 32),), jnp.float32),
    }


def reference(gradient, error, momentum, q_init):
    highest = lax.Precision.HIGHEST
    compensated = gradient.astype(jnp.float32) + error.astype(jnp.float32)
    basis = q_init
    ortho = jnp.zeros((compensated.shape[1], basis.shape[1]), jnp.float32)
    for step in range(ITERS):
        summed = jnp.einsum('dmc,cr->mr', compensated, basis, precision=highest)
        gram = jnp.dot(summed.T, summed, precision=highest)
        lower = jnp.linalg.cholesky(gram)
        ortho = lax.linalg.triangular_solve(lower, summed, left_side=False, lower=True, transpose_a=True)
        basis = jnp.einsum('dmc,mr->cr', compensated, ortho, precision=highest) / REPL
    update = jnp.dot(ortho, basis.T, precision=highest)
    new_error = (compensated - update[None]).astype(jnp.bfloat16)
    new_momentum = (0.9 * momentum.astype(jnp.float32) + update).astype(jnp.bfloat16)
    return (new_error, new_momentum, basis)
```

```python
import jax
import jax.numpy as jnp
from jax import lax
from jax.sharding import PartitionSpec as P

ITERS = 2
N_DP = 8
N_MP = 32
N_Y = 4
N_X = 4
N_Z = 8
PIECE = 32
HIGHEST = lax.Precision.HIGHEST

CORE = [(i, i ^ 1) for i in range(N_DP)]


def y_shift(k):
    return [(i, (i + 2 * k) % N_DP) for i in range(N_DP)]


def x_shift(k):
    return [(i, i // N_X * N_X + (i + k) % N_X) for i in range(N_MP)]


def dp_send(value, pairs):
    return lax.ppermute(value, "dp", pairs)


def mm(a, b):
    return jnp.dot(a, b, precision=HIGHEST)


def mm_t(a, b):
    return lax.dot_general(a, b, (((0,), (0,)), ((), ())), precision=HIGHEST)


def reduce_replicas(gradient, error, y, c):
    rows, cols = gradient.shape
    width = cols // N_DP
    half = rows // 2

    def block(k, core):
        start = (2 * ((y + k) % N_Y) + core) * width
        g = lax.dynamic_slice_in_dim(gradient, start, width, 1)
        e = lax.dynamic_slice_in_dim(error, start, width, 1)
        return g.astype(jnp.float32) + e.astype(jnp.float32)

    parts = {}
    for k in (2, 1, 3, 0):
        parts[k] = block(k, c) + dp_send(block(k, 1 - c), CORE)
    up, down = y_shift(1), y_shift(-1)
    far_a = dp_send(parts[2][:half], up)
    far_b = dp_send(parts[2][half:], down)
    up_b = dp_send(parts[1][half:], up)
    down_a = dp_send(parts[3][:half], down)
    up_a = dp_send(parts[1][:half] + far_a, up)
    down_b = dp_send(parts[3][half:] + far_b, down)
    return jnp.concatenate([parts[0][:half] + up_a + down_a, parts[0][half:] + up_b + down_b], 0)


def spread_q(q_init, dp, z):
    value = q_init
    for hop in (4, 2, 1):
        pairs = []
        for j in range(N_DP):
            for s in range(0, N_Z, 2 * hop):
                for x in range(N_X):
                    src, dst = (j + s) % N_Z, (j + s + hop) % N_Z
                    pairs.append((j * N_MP + src * N_X + x, j * N_MP + dst * N_X + x))
        got = lax.ppermute(value, ("dp", "mp"), pairs)
        value = jnp.where((z - dp) % (2 * hop) == hop, got, value)
    return value


def gather_x(value, x):
    rows = value.shape[0]
    out = jnp.zeros((N_X * rows, value.shape[1]), value.dtype)
    out = lax.dynamic_update_slice_in_dim(out, value, x * rows, 0)
    for k in (1, 2, 3):
        got = lax.ppermute(value, "mp", x_shift(k))
        out = lax.dynamic_update_slice_in_dim(out, got, (x - k) % N_X * rows, 0)
    return out


def sum_over_dp(value, c):
    half = value.shape[0] // 2
    mine = lax.dynamic_slice_in_dim(value, c * half, half, 0)
    theirs = lax.dynamic_slice_in_dim(value, (1 - c) * half, half, 0)
    mine = mine + dp_send(theirs, CORE)
    total = mine
    for k in (2, 1, 3):
        total = total + dp_send(mine, y_shift(k))
    other = dp_send(total, CORE)
    first = jnp.where(c == 0, total, other)
    second = jnp.where(c == 0, other, total)
    return jnp.concatenate([first, second], 0)


def sum_over_mp(terms, gram):
    rows, rank = terms.shape
    pad = jnp.zeros((N_MP * PIECE - rows - gram.shape[0], rank), jnp.float32)
    packed = jnp.concatenate([terms, gram, pad], 0).reshape(N_MP, PIECE, rank)
    got = lax.all_to_all(packed, "mp", 0, 0)
    own = jnp.sum(got, 0)
    full = lax.all_to_all(jnp.broadcast_to(own[None], packed.shape), "mp", 0, 0)
    full = full.reshape(N_MP * PIECE, rank)
    return full[:rows], full[rows : rows + gram.shape[0]]


def inverse_factor(gram):
    lower = jnp.linalg.cholesky(gram)
    eye = jnp.eye(gram.shape[0], dtype=jnp.float32)
    return lax.linalg.triangular_solve(lower, eye, left_side=True, lower=True)


def gather_dp(value, y, c):
    rows, rank = value.shape
    half = rows // 2
    up, down = y_shift(1), y_shift(-1)
    a, b = value[:half], value[half:]
    prev_a, next_b = dp_send(a, up), dp_send(b, down)
    prev_b, next_a = dp_send(b, up), dp_send(a, down)
    far_a, far_b = dp_send(prev_a, up), dp_send(next_b, down)
    out = jnp.zeros((N_Y, 2, half, rank), jnp.float32)
    for k, pair in ((0, (a, b)), (3, (prev_a, prev_b)), (1, (next_a, next_b)), (2, (far_a, far_b))):
        out = lax.dynamic_update_slice(out, jnp.stack(pair)[None], ((y + k) % N_Y, 0, 0, 0))
    own = out.reshape(N_Y, rows, rank)
    other = dp_send(own, CORE)
    both = jnp.where(c == 0, jnp.stack([own, other], 1), jnp.stack([other, own], 1))
    return both.reshape(N_DP * rows, rank)


def body(gradient, error, momentum, q_init):
    gradient, error = gradient[0], error[0]
    dp, mp = lax.axis_index("dp"), lax.axis_index("mp")
    y, c = dp // 2, dp % 2
    z, x = mp // N_X, mp % N_X
    shard_rows = q_init.shape[0]

    total = reduce_replicas(gradient, error, y, c)
    basis = gather_x(spread_q(q_init, dp, z), x)

    summed = sum_over_dp(mm(total, basis), c)
    terms, gram = sum_over_mp(mm_t(total, summed), mm_t(summed, summed))
    product = sum_over_dp(mm(total, terms), c)
    inverse = inverse_factor(gram)
    summed = lax.dot_general(product, inverse, (((1,), (1,)), ((), ())), precision=HIGHEST) / N_DP

    terms, gram = sum_over_mp(mm_t(total, summed), mm_t(summed, summed))
    inverse = inverse_factor(gram)
    terms = gather_dp(terms, y, c)
    ortho = lax.dot_general(summed, inverse, (((1,), (1,)), ((), ())), precision=HIGHEST)
    left = mm(ortho, inverse) / N_DP
    update = lax.dot_general(left, terms, (((1,), (1,)), ((), ())), precision=HIGHEST)

    compensated = gradient.astype(jnp.float32) + error.astype(jnp.float32)
    new_error = (compensated - update).astype(jnp.bfloat16)[None]
    new_momentum = (0.9 * momentum.astype(jnp.float32) + update).astype(jnp.bfloat16)
    own_terms = lax.dynamic_slice_in_dim(terms, mp * shard_rows, shard_rows, 0)
    new_q = lax.dot_general(own_terms, inverse, (((1,), (1,)), ((), ())), precision=HIGHEST) / N_DP
    return (new_error, new_momentum, new_q)


def solution(mesh):
    return jax.shard_map(
        body,
        mesh=mesh,
        in_specs=(P("dp", "mp", None), P("dp", "mp", None), P("mp", None), P("mp", None)),
        out_specs=(P("dp", "mp", None), P("mp", None), P("mp", None)),
        check_vma=False,
    )
```
